128 devices in a mesh: inp: 8 (over x_lo, z), wt: 4 (over x_hi, core), out: 4 (over y).
Axes of the slice: x: 4 (x_hi: 2, x_lo: 2; x = x_hi * 2 + x_lo), y: 4, z: 4, core: 2. Of those that a mesh axis runs over, the one named last changes fastest.
Arguments:
- tokens: bfloat16 [1024, 8192], P(('wt', 'inp'), 'out'), may hold values from -6 to 6
- out_grad: bfloat16 [1024, 8192], P(('wt', 'inp'), 'out'), may hold values from -1.5 to 1.5
- gate_weight: bfloat16 [8192, 14336], P(('out', 'wt'), 'inp'), may hold values from -0.0625 to 0.0625
- up_weight: bfloat16 [8192, 14336], P(('out', 'wt'), 'inp'), may hold values from -0.0625 to 0.0625
- down_weight: bfloat16 [8192, 14336], P(('out', 'wt'), 'inp'), may hold values from -0.046875 to 0.046875
Outputs:
- input_grad: bfloat16 [1024, 8192], P(('wt', 'inp'), 'out')
- gate_grad: bfloat16 [8192, 14336], P(('out', 'wt'), 'inp')
- up_grad: bfloat16 [8192, 14336], P(('out', 'wt'), 'inp')
- down_grad: bfloat16 [8192, 14336], P(('out', 'wt'), 'inp')
The draws below stay inside these ranges and needn't reach their ends.
All inputs are finite; a program needn't handle non-finite values.
Results may differ from the reference program's by a relative error of at most 0.03.
Values may be sent and summed in bfloat16 or wider, within the bound.
A program may use at most 128 MiB of HBM per device.

```python
import jax
import jax.numpy as jnp
from jax import lax

D = 8192
FF = 14336
TOKENS = 1024
N_WT = 4
N_OUT = 4


def block_scale(rng, extent, cuts, smallest, largest):
    loudness, own = 1.0, jax.random.fold_in(rng, 6)
    for position, parts in cuts:
        draws = jnp.exp(jax.random.uniform(jax.random.fold_in(own, position), (parts,), jnp.float32, smallest / len(cuts), largest / len(cuts)))
        loudness = loudness * jnp.repeat(draws, extent[position] // parts).reshape([-1 if axis == position else 1 for axis in range(len(extent))])
    return loudness


def centred(stream_key, shape, spread, reach, cuts=(), held_as=jnp.bfloat16):
    loudness = block_scale(stream_key, shape, cuts, -0.22, 0.18) if cuts else 1.0
    array = jax.random.normal(stream_key, shape, jnp.float32) * spread * loudness
    return jnp.minimum(jnp.maximum(array, -reach), reach).astype(held_as)


def setup_inputs(seed: int = 0) -> dict:
    arg_keys = jax.random.split(jax.random.key(seed), 6)
    tokens = centred(arg_keys[0], (TOKENS, D), 1.0, 6.0, ((0, 32), (1, 4)))
    out_grad = centred(arg_keys[1], (TOKENS, D), 0.25, 1.5, ((0, 32), (1, 4)))
    gate_weight = centred(arg_keys[2], (D, FF), D ** -0.5, 0.0625, ((0, 16), (1, 8)))
    up_weight = centred(arg_keys[3], (D, FF), D ** -0.5, 0.0625, ((0, 16), (1, 8)))
    down_weight = centred(arg_keys[4], (D, FF), FF ** -0.5, 0.046875, ((0, 16), (1, 8)))
    return {"tokens": tokens, "out_grad": out_grad, "gate_weight": gate_weight, "up_weight": up_weight, "down_weight": down_weight}


def feature_blocked(left, right, blocks):
    width = left.shape[1] // blocks
    total = jnp.zeros((left.shape[0], right.shape[1]), jnp.float32)
    for block in range(blocks):
        part = jnp.dot(left[:, block * width:(block + 1) * width], right[block * width:(block + 1) * width], preferred_element_type=jnp.float32)
        part = lax.optimization_barrier(part.astype(jnp.bfloat16))
        total = total + part.astype(jnp.float32)
    return total


def token_blocked(left, right, blocks):
    height = left.shape[0] // blocks
    total = jnp.zeros((left.shape[1], right.shape[1]), jnp.float32)
    for block in range(blocks):
        part = jnp.dot(left[block * height:(block + 1) * height].T, right[block * height:(block + 1) * height], preferred_element_type=jnp.float32)
        part = lax.optimization_barrier(part.astype(jnp.bfloat16))
        total = total + part.astype(jnp.float32)
    return total


def reference(tokens, out_grad, gate_weight, up_weight, down_weight):
    gate = feature_blocked(tokens, gate_weight, N_OUT)
    up = feature_blocked(tokens, up_weight, N_OUT)
    hidden_grad = feature_blocked(out_grad, down_weight, N_OUT)
    sigma = jax.nn.sigmoid(gate)
    active = gate * sigma
    hidden = (active * up).astype(jnp.bfloat16)
    up_delta = (hidden_grad * active).astype(jnp.bfloat16)
    gate_delta = (hidden_grad * up * sigma * (1.0 + gate * (1.0 - sigma))).astype(jnp.bfloat16)
    input_grad = jnp.dot(gate_delta, gate_weight.T, preferred_element_type=jnp.float32) + jnp.dot(up_delta, up_weight.T, preferred_element_type=jnp.float32)
    gate_grad = token_blocked(tokens, gate_delta, N_WT).astype(jnp.bfloat16)
    up_grad = token_blocked(tokens, up_delta, N_WT).astype(jnp.bfloat16)
    down_grad = token_blocked(out_grad, hidden, N_WT).astype(jnp.bfloat16)
    return input_grad.astype(jnp.bfloat16), gate_grad, up_grad, down_grad
```

```python
import functools

import jax
import jax.numpy as jnp
from jax import lax
from jax.experimental import pallas as pl
from jax.experimental.pallas import tpu as pltpu
from jax.sharding import PartitionSpec as P

BF16 = jnp.bfloat16
F32 = jnp.float32
MESH = pl.DeviceIdType.MESH
N_SEM = 208

ORDER = (
    ("T1", 0), ("T1", 1), ("F", 0), ("TR", 0), ("A1", 0), ("T2", 0), ("F", 1), ("F", 2), ("B1", 0), ("A2", 0),
    ("TR", 1), ("T3", 0), ("A1", 1), ("TR", 2), ("F", 3), ("B1", 1), ("A1", 2), ("TR", 3), ("B2", 0), ("A2", 1),
    ("B1", 2), ("A1", 3), ("A3", 0), ("B2", 1), ("A2", 2), ("B3", 0), ("B1", 3), ("B2", 2), ("A3", 1), ("A3s", 1),
    ("A2", 3), ("A3", 2), ("B3", 1), ("B2", 3), ("B3s", 1), ("A3s", 2), ("B3", 2), ("A4", 1), ("B3s", 2), ("A3", 3),
    ("B3", 3), ("A3s", 3), ("B3s", 3), ("A3s", 0), ("B3s", 0), ("B4", 1), ("A4", 2), ("A5", 1), ("A4", 3), ("B4", 2),
    ("A4", 0), ("B4", 3), ("B4", 0), ("B5", 1), ("A5", 2), ("A5", 3), ("B5", 2), ("A5", 0), ("B5", 3), ("B5", 0),
    ("C", 1), ("G", 1), ("C", 2), ("C", 3), ("G", 2), ("I3", 0), ("I12", 0), ("G", 3), ("C", 0), ("I12b", 0),
    ("I0", 0), ("G", 0), ("I0f", 0),
)


def kernel(
    tok_in, og_in, wg_in, wu_in, wd_in, ig_out, gg_out, ug_out, dg_out,
    w, tok, ttr, pp, pq, r1p, r1q, r2p, r2q, rxp, rxq, dp, dq, acc, go, ig, rigc, rz1, rz2, rix, igo,
    ssem, rsem, lsem,
):
    inp, wt, y = lax.axis_index("inp"), lax.axis_index("wt"), lax.axis_index("out")
    xl, z, xh, c = inp // 4, inp % 4, wt // 2, wt % 2
    yn, yp, yo = (y + 1) % 4, (y + 3) % 4, (y + 2) % 4
    oxh, oxl, oc = 1 - xh, 1 - xl, 1 - c
    core = {"wt": xh * 2 + oc}
    x2 = {"wt": oxh * 2 + c}
    xlp = {"inp": oxl * 4 + z}
    diag = {"inp": oxl * 4 + z, "wt": oxh * 2 + c}
    zn, zp = {"inp": xl * 4 + (z + 1) % 4}, {"inp": xl * 4 + (z + 3) % 4}
    ynd, ypd = {"out": yn}, {"out": yp}
    feats, half = w.shape[1], w.shape[2]
    own_f = feats // 2
    p_cols, q_cols = pp.shape[-1], pq.shape[-1]
    rows = tok.shape[-2]
    chunk = 8 * rows
    hr = rows // 2
    cols = lambda h: pl.ds(pl.multiple_of(h * feats, 128), feats)
    hcols = lambda h: pl.ds(pl.multiple_of(h * half, 128), half)
    frows = lambda h: pl.ds(pl.multiple_of(h * own_f, 16), own_f)

    arrivals, all_sends = {}, []

    def send(name, src, dst, device):
        i = len(all_sends)
        assert i < N_SEM
        cp = pltpu.make_async_remote_copy(
            src_ref=src, dst_ref=dst, send_sem=ssem.at[i], recv_sem=rsem.at[i], device_id=device, device_id_type=MESH
        )
        cp.start()
        all_sends.append(cp)
        arrivals[name] = cp

    def arrive(*name):
        arrivals.pop(name).wait_recv()

    local = []

    def bring(src, dst):
        cp = pltpu.make_async_copy(src, dst, lsem.at[len(local)])
        cp.start()
        local.append(cp)

    acts = (tok_in, og_in)
    weights = (wg_in, wu_in, wd_in)
    for a in (0, 1):
        bring(acts[a].at[:, cols(xh)], tok.at[0, xh, c, xl, a])
    for a in range(3):
        bring(weights[a].at[:, hcols(c)], w.at[a, frows(c), :])

    barrier = pltpu.get_barrier_semaphore()
    for device in (core, x2, xlp, diag, zn, zp, ynd, ypd):
        pl.semaphore_signal(barrier, inc=1, device_id=device, device_id_type=MESH)
    pl.semaphore_wait(barrier, 8)

    near = (("xlp", xlp, xh, xh, oxl), ("diag", diag, oxh, oxh, oxl), ("x2", x2, oxh, oxh, xl))
    for a in (0, 1):
        for name, device, h, _, _ in near:
            send(("x0", name, a), acts[a].at[:, cols(h)], tok.at[0, xh, c, xl, a], device)
    for a in (0, 1):
        mine = acts[a].at[:, cols(xh)]
        send(("c0", "own", a), mine, tok.at[0, xh, c, xl, a], core)
    for a in range(3):
        send(("w", a), weights[a].at[:, hcols(oc)], w.at[a, frows(c), :], core)
    for a in (0, 1):
        mine = acts[a].at[:, cols(xh)]
        send(("zn", "own", a), mine, tok.at[2, xh, c, xl, a], zn)
        send(("zp", "own", a), mine, tok.at[1, xh, c, xl, a], zp)

    def T1(a):
        for name, _, _, sxh, sxl in near:
            arrive("x0", name, a)
            block = tok.at[0, sxh, c, sxl, a]
            send(("c0", name, a), block, block, core)
            send(("zn", name, a), block, tok.at[2, sxh, c, sxl, a], zn)
            send(("zp", name, a), block, tok.at[1, sxh, c, sxl, a], zp)

    def T2(_):
        for way in ("zn", "zp"):
            for name in ("own", "xlp", "diag", "x2"):
                for a in (0, 1):
                    arrive(way, name, a)
        send(("zf", 0), tok.at[2, 0, c], tok.at[3, 0, c], zn)
        send(("zf", 1), tok.at[1, 1, c], tok.at[3, 1, c], zp)
        for k in (1, 2):
            send(("ck", k), tok.at[k, :, c], tok.at[k, :, c], core)

    def T3(_):
        for h in (0, 1):
            arrive("zf", h)
            send(("ck3", h), tok.at[3, h, c], tok.at[3, h, c], core)

    def project(k, a):
        left = tok[k, :, :, :, a // 2].reshape(chunk, feats)
        pp[k, :, :, a] = jnp.dot(left, w[a, :, :p_cols], preferred_element_type=F32).astype(BF16).reshape(4, 2, rows, p_cols)
        pq[k, :, :, a] = jnp.dot(left, w[a, :, p_cols:], preferred_element_type=F32).astype(BF16).reshape(4, 2, rows, q_cols)

    def F(k):
        if k == 0:
            for a in (0, 1):
                local[a].wait()
                for name in ("own", "xlp", "diag", "x2"):
                    arrive("c0", name, a)
            for a in range(3):
                local[2 + a].wait()
                arrive("w", a)
        elif k == 3:
            arrive("ck3", 0)
            arrive("ck3", 1)
        else:
            arrive("ck", k)

        @pl.loop(0, 3)
        def _(a):
            project(k, a)

        send(("s1", k, 0), pp.at[k, yo, 0], r1p.at[k, 0], ynd)
        send(("s1", k, 1), pp.at[k, yo, 1], r1p.at[k, 1], ypd)
        for j, t in enumerate((yo, yn, yp, y)):
            send(("qx", k, j), pq.at[k, t, oxh], rxq.at[k, t], x2)
        send(("s2", k, 0, 1), pp.at[k, yn, 1], r2p.at[k, 0, 1], ynd)
        send(("s2", k, 1, 0), pp.at[k, yp, 0], r2p.at[k, 1, 0], ypd)

    def add(ref, *others):
        total = ref[...].astype(F32)
        for other in others:
            total += other[...].astype(F32)
        return total

    def A1(k):
        for way, t, device in ((0, yn, ynd), (1, yp, ypd)):
            arrive("s1", k, way)
            ref = pp.at[k, t, way]
            ref[...] = add(ref, r1p.at[k, way]).astype(BF16)
            send(("s2", k, way, way), ref, r2p.at[k, way, way], device)

    def B1(k):
        for j, t in enumerate((yo, yn, yp, y)):
            arrive("qx", k, j)
            ref = pq.at[k, t, xh]
            ref[...] = add(ref, rxq.at[k, t]).astype(BF16)
            if j == 0:
                send(("t1", k, 0), ref.at[:, :hr], r1q.at[k, 0], ynd)
                send(("t1", k, 1), ref.at[:, hr:], r1q.at[k, 1], ypd)
            if j == 1:
                send(("t2", k, 0, 1), ref.at[:, hr:], r2q.at[k, 0, :, hr:], ynd)
            if j == 2:
                send(("t2", k, 1, 0), ref.at[:, :hr], r2q.at[k, 1, :, :hr], ypd)

    def B2(k):
        for way, t, device in ((0, yn, ynd), (1, yp, ypd)):
            arrive("t1", k, way)
            part = slice(0, hr) if way == 0 else slice(hr, rows)
            ref = pq.at[k, t, xh, :, part]
            ref[...] = add(ref, r1q.at[k, way]).astype(BF16)
            send(("t2", k, way, way), ref, r2q.at[k, way, :, part], device)

    def A2(k):
        for way in (0, 1):
            for h in (0, 1):
                arrive("s2", k, way, h)
        ref = pp.at[k, y, oxh]
        ref[...] = add(ref, r2p.at[k, 0, oxh], r2p.at[k, 1, oxh]).astype(BF16)
        send(("rx", k), ref, rxp.at[k], x2)

    def activate(sums, out):
        gate, up, hidden_grad = sums[0], sums[1], sums[2]
        sigma = jax.nn.sigmoid(gate)
        active = gate * sigma
        out[0] = (hidden_grad * up * sigma * (1.0 + gate * (1.0 - sigma))).astype(BF16)
        out[1] = (hidden_grad * active).astype(BF16)
        out[2] = (active * up).astype(BF16)

    def A3(k):
        arrive("rx", k)
        activate(add(pp.at[k, y, xh], r2p.at[k, 0, xh], r2p.at[k, 1, xh], rxp.at[k]), dp.at[k, y, xh])

    def A3s(k):
        ref = dp.at[k, y, xh]
        send(("dx", k), ref, ref, x2)
        send(("do", k, 0), ref, ref, ynd)
        send(("do", k, 1), ref, ref, ypd)

    def B3(k):
        for way in (0, 1):
            for h in (0, 1):
                arrive("t2", k, way, h)
        activate(add(pq.at[k, y, xh], r2q.at[k, 0], r2q.at[k, 1]), dq.at[k, y, xh])

    def B3s(k):
        ref = dq.at[k, y, xh]
        send(("eo", k, 0), ref, ref, ynd)
        send(("eo", k, 1), ref, ref, ypd)
        send(("ex", k, 0), ref, ref, x2)

    def A4(k):
        arrive("dx", k)
        ref = dp.at[k, y, oxh]
        send(("dt", k, 0), ref, ref, ynd)
        send(("dt", k, 1), ref, ref, ypd)

    def A5(k):
        arrive("do", k, 0)
        ref = dp.at[k, yp, xh]
        send(("df", k, 0), ref, ref, ynd)
        arrive("dt", k, 1)
        ref = dp.at[k, yn, oxh]
        send(("df", k, 1), ref, ref, ypd)

    def B4(k):
        arrive("eo", k, 0)
        ref = dq.at[k, yp, xh, :, :hr]
        send(("ef", k, 0), ref, ref, ynd)
        arrive("eo", k, 1)
        ref = dq.at[k, yn, xh, :, hr:]
        send(("ef", k, 1), ref, ref, ypd)
        for j, t in ((1, yp), (2, yn)):
            ref = dq.at[k, t, xh]
            send(("ex", k, j), ref, ref, x2)

    def B5(k):
        arrive("ef", k, 0)
        arrive("ef", k, 1)
        ref = dq.at[k, yo, xh]
        send(("ex", k, 3), ref, ref, x2)

    def TR(k):
        @pl.loop(0, 2)
        def _(a):
            ttr[a, k] = tok[k, :, :, :, a].reshape(chunk, feats).T

    def C(k):
        for name in (("df", k, 0), ("df", k, 1), ("dt", k, 0), ("do", k, 1), ("ex", k, 0), ("ex", k, 1), ("ex", k, 2), ("ex", k, 3)):
            arrive(*name)
        nt = (((1,), (1,)), ((), ()))

        @pl.loop(0, 2)
        def _(j):
            fr = pl.ds(pl.multiple_of(j * own_f, 128), own_f)
            total = jnp.zeros((chunk, own_f), F32)
            for a in (0, 1):
                left = dp[k, :, :, a].reshape(chunk, p_cols)
                total += lax.dot_general(left, w[a, fr, :p_cols], nt, preferred_element_type=F32)
                left = dq[k, :, :, a].reshape(chunk, q_cols)
                total += lax.dot_general(left, w[a, fr, p_cols:], nt, preferred_element_type=F32)
            ig[k, :, :, :, :, fr] = total.astype(BF16).reshape(2, 2, 2, rows, own_f)

        send(("igc", k), ig.at[k, :, oc], rigc.at[k], core)

    def gradient(k, a, part, first, last):
        left = ttr[a // 2, k, part, :]
        for ref, lanes in ((dp, slice(0, p_cols)), (dq, slice(p_cols, half))):
            right = ref[k, :, :, a].reshape(chunk, ref.shape[-1])
            value = jnp.dot(left, right, preferred_element_type=F32)
            if not first:
                value += acc[a, part, lanes]
            if last:
                go[a, part, lanes] = value.astype(BF16)
            else:
                acc[a, part, lanes] = value

    outs = (gg_out, ug_out, dg_out)

    def G(k):
        first, last = k == 1, k == 0
        if not last:
            @pl.loop(0, 6)
            def _(i):
                gradient(k, i // 2, pl.ds(pl.multiple_of((i % 2) * own_f, 128), own_f), first, last)
        else:
            for h, remote in ((oc, True), (c, False)):
                for a in range(3):
                    gradient(k, a, frows(h), first, last)
                    if remote:
                        send(("go", a), go.at[a, frows(h), :], outs[a].at[:, hcols(c)], core)
                    else:
                        bring(go.at[a, frows(h), :], outs[a].at[:, hcols(c)])

    def both(k, h):
        return ig[k, h, c].astype(F32) + rigc[k, h].astype(F32)

    def I3(_):
        arrive("igc", 3)
        for h in (0, 1):
            ref = ig.at[3, h, c]
            ref[...] = both(3, h).astype(BF16)
            send(("z1", h), ref, rz1.at[h], zn if h == 0 else zp)

    def I12(_):
        for k, device, way in ((1, zn, 0), (2, zp, 1)):
            arrive("igc", k)
            h = 1 - way
            ref = ig.at[k, h, c]
            ref[...] = both(k, h).astype(BF16)
            send(("z2", way, h), ref, rz2.at[way, h], device)

    def I12b(_):
        for k, device, way in ((1, zn, 0), (2, zp, 1)):
            arrive("z1", way)
            ref = ig.at[k, way, c]
            ref[...] = (both(k, way) + rz1[way].astype(F32)).astype(BF16)
            send(("z2", way, way), ref, rz2.at[way, way], device)

    def I0(_):
        arrive("igc", 0)
        for h in (0, 1):
            for way in (0, 1):
                arrive("z2", way, h)
            ig[0, h, c] = (both(0, h) + rz2[0, h].astype(F32) + rz2[1, h].astype(F32)).astype(BF16)
        send(("ix", 0), ig.at[0, xh, c, oxl], rix.at[0], xlp)
        send(("ix", 1), ig.at[0, oxh, c, oxl], rix.at[1], diag)
        send(("ix", 2), ig.at[0, oxh, c, xl], rix.at[2], x2)

    def I0f(_):
        for j in range(3):
            arrive("ix", j)
        igo[:, cols(xh)] = (ig[0, xh, c, xl].astype(F32) + rix[0].astype(F32)).astype(BF16)
        igo[:, cols(oxh)] = (rix[1].astype(F32) + rix[2].astype(F32)).astype(BF16)
        bring(igo, ig_out)

    steps = dict(
        T1=T1, T2=T2, T3=T3, F=F, A1=A1, B1=B1, B2=B2, A2=A2, A3=A3, A3s=A3s, B3=B3, B3s=B3s, A4=A4, A5=A5, B4=B4,
        B5=B5, TR=TR, C=C, G=G, I3=I3, I12=I12, I12b=I12b, I0=I0, I0f=I0f,
    )
    for step, k in ORDER:
        steps[step](k)
    for a in range(3):
        arrive("go", a)
    for cp in local[5:]:
        cp.wait()
    for cp in all_sends:
        cp.wait_send()
    assert not arrivals, "left over"


def on_device(tokens, out_grad, gate_weight, up_weight, down_weight):
    rows, model = tokens.shape
    own_f, hidden = gate_weight.shape
    feats, half = 2 * own_f, hidden // 2
    q_cols = (half // 128 * 3 // 7) * 128
    p_cols = half - q_cols
    hr = rows // 2
    vmem = lambda *shape: pltpu.VMEM(shape, BF16)
    any_spec = pl.BlockSpec(memory_space=pl.ANY)
    out_shapes = [tokens, gate_weight, up_weight, down_weight]
    return pl.pallas_call(
        kernel,
        out_shape=[jax.ShapeDtypeStruct(o.shape, BF16) for o in out_shapes],
        in_specs=[any_spec] * 5,
        out_specs=[any_spec] * 4,
        scratch_shapes=[
            vmem(3, feats, half),
            vmem(4, 2, 2, 2, 2, rows, feats),
            vmem(2, 4, feats, 8 * rows),
            vmem(4, 4, 2, 3, rows, p_cols),
            vmem(4, 4, 2, 3, rows, q_cols),
            vmem(4, 2, 3, rows, p_cols),
            vmem(4, 2, 3, hr, q_cols),
            vmem(4, 2, 2, 3, rows, p_cols),
            vmem(4, 2, 3, rows, q_cols),
            vmem(4, 3, rows, p_cols),
            vmem(4, 4, 3, rows, q_cols),
            vmem(4, 4, 2, 3, rows, p_cols),
            vmem(4, 4, 2, 3, rows, q_cols),
            pltpu.VMEM((3, feats, half), F32),
            vmem(3, feats, half),
            vmem(4, 2, 2, 2, rows, feats),
            vmem(4, 2, 2, rows, feats),
            vmem(2, 2, rows, feats),
            vmem(2, 2, 2, rows, feats),
            vmem(3, rows, feats),
            vmem(rows, model),
            pltpu.SemaphoreType.DMA((N_SEM,)),
            pltpu.SemaphoreType.DMA((N_SEM,)),
            pltpu.SemaphoreType.DMA((16,)),
        ],
        compiler_params=pltpu.CompilerParams(
            collective_id=0, has_side_effects=True, vmem_limit_bytes=60 * 2**20
        ),
        cost_estimate=pl.CostEstimate(flops=15 * 10**9, bytes_accessed=12 * 2**20, transcendentals=10**6),
    )(tokens, out_grad, gate_weight, up_weight, down_weight)


def solution(mesh):
    in_specs = (
        P(("wt", "inp"), "out"),
        P(("wt", "inp"), "out"),
        P(("out", "wt"), "inp"),
        P(("out", "wt"), "inp"),
        P(("out", "wt"), "inp"),
    )
    out_specs = (
        P(("wt", "inp"), "out"),
        P(("out", "wt"), "inp"),
        P(("out", "wt"), "inp"),
        P(("out", "wt"), "inp"),
    )
    return jax.shard_map(
        on_device, mesh=mesh, in_specs=in_specs, out_specs=out_specs, check_vma=False
    )
```

```python
import functools

import jax
import jax.numpy as jnp
from jax import lax
from jax.experimental import pallas as pl
from jax.experimental.pallas import tpu as pltpu
from jax.sharding import PartitionSpec as P

BF16 = jnp.bfloat16
F32 = jnp.float32
MESH = pl.DeviceIdType.MESH
N_SEM = 208

ORDER = (
    ("T1", 0), ("F", 0, 0), ("T1", 1), ("F", 0, 1), ("A1", 0), ("T2", 0), ("B1a", 0), ("B1b", 0), ("F", 1),
    ("F", 2), ("A1", 1), ("T3", 0), ("B1a", 1), ("F", 3), ("A2", 1), ("B1b", 1), ("B2", 1), ("B1a", 2), ("A1", 3),
    ("B1b", 2), ("B2", 2), ("A2", 0), ("A1", 2), ("B2", 0), ("B3", 1), ("A2", 3), ("B1a", 3), ("B3y", 1),
    ("B1b", 3), ("A3", 1), ("A3x", 1), ("A2", 2), ("B2", 3), ("B3x", 1), ("A3", 0), ("A3y", 1), ("A3", 3),
    ("A3y", 3), ("B3", 2), ("A3x", 3), ("B4y", 1), ("B3", 3), ("A3", 2), ("B4x", 1), ("B3x", 3), ("B3y", 2),
    ("A4", 1), ("B3y", 3), ("A4", 3), ("B5", 1), ("A5b", 1), ("B4y", 2), ("A3x", 2), ("A5a", 1), ("B4x", 2),
    ("B4y", 3), ("A3y", 2), ("B4x", 3), ("A4", 2), ("A5a", 3), ("B5", 3), ("A3x", 0), ("B3", 0), ("A5b", 3),
    ("B5", 2), ("B3y", 0), ("C", 1), ("B3x", 2), ("B3x", 0), ("G", 1), ("A5b", 2), ("A5a", 2), ("A3y", 0), ("C", 3),
    ("B4y", 0), ("A4", 0), ("G", 3), ("I3", 0), ("B4x", 0), ("C", 2), ("A5a", 0), ("I12", 0), ("B5", 0), ("A5b", 0),
    ("I12b", 0), ("G", 2), ("C", 0), ("I0", 0), ("G", 0), ("I0f", 0),
)


def kernel(
    tok_in, og_in, wg_in, wu_in, wd_in, ig_out, gg_out, ug_out, dg_out,
    w, tok, ttr, pp, pq, r1p, r1q, r2p, r2q, rxp, rxq, dp, dq, acc, go, ig, rigc, rz1, rz2, rix,
    ssem, rsem, lsem,
):
    inp, wt, y = lax.axis_index("inp"), lax.axis_index("wt"), lax.axis_index("out")
    xl, z, xh, c = inp // 4, inp % 4, wt // 2, wt % 2
    yn, yp, yo = (y + 1) % 4, (y + 3) % 4, (y + 2) % 4
    oxh, oxl, oc = 1 - xh, 1 - xl, 1 - c
    core = {"wt": xh * 2 + oc}
    x2 = {"wt": oxh * 2 + c}
    xlp = {"inp": oxl * 4 + z}
    diag = {"inp": oxl * 4 + z, "wt": oxh * 2 + c}
    zn, zp = {"inp": xl * 4 + (z + 1) % 4}, {"inp": xl * 4 + (z + 3) % 4}
    ynd, ypd = {"out": yn}, {"out": yp}
    feats, half = w.shape[1], w.shape[2]
    own_f = feats // 2
    p_cols, q_cols = pp.shape[-1], pq.shape[-1]
    rows = tok.shape[-2]
    chunk = 8 * rows
    hr = rows // 2
    cols = lambda h: pl.ds(pl.multiple_of(h * feats, 128), feats)
    hcols = lambda h: pl.ds(pl.multiple_of(h * half, 128), half)
    frows = lambda h: pl.ds(pl.multiple_of(h * own_f, 16), own_f)

    arrivals, all_sends = {}, []

    def send(name, src, dst, device):
        i = len(all_sends)
        assert i < N_SEM
        cp = pltpu.make_async_remote_copy(
            src_ref=src, dst_ref=dst, send_sem=ssem.at[i], recv_sem=rsem.at[i], device_id=device, device_id_type=MESH
        )
        cp.start()
        all_sends.append(cp)
        arrivals[name] = cp

    def arrive(*name):
        arrivals.pop(name).wait_recv()

    local = []

    def bring(src, dst):
        cp = pltpu.make_async_copy(src, dst, lsem.at[len(local)])
        cp.start()
        local.append(cp)

    acts = (tok_in, og_in)
    outs = (gg_out, ug_out, dg_out)
    weights = (wg_in, wu_in, wd_in)
    for a in (0, 1):
        bring(acts[a].at[:, cols(xh)], tok.at[0, xh, c, xl, a])
    for a in range(3):
        bring(weights[a].at[:, hcols(c)], w.at[a, frows(c), :])

    barrier = pltpu.get_barrier_semaphore()
    for device in (core, x2, xlp, diag, zn, zp, ynd, ypd):
        pl.semaphore_signal(barrier, inc=1, device_id=device, device_id_type=MESH)
    pl.semaphore_wait(barrier, 8)

    near = (("xlp", xlp, xh, xh, oxl), ("diag", diag, oxh, oxh, oxl), ("x2", x2, oxh, oxh, xl))
    for a in (0, 1):
        for name, device, h, _, _ in near:
            send(("x0", name, a), acts[a].at[:, cols(h)], tok.at[0, xh, c, xl, a], device)
    for a in (0, 1):
        mine = acts[a].at[:, cols(xh)]
        send(("c0", "own", a), mine, tok.at[0, xh, c, xl, a], core)
    for a in range(3):
        send(("w", a), weights[a].at[:, hcols(oc)], w.at[a, frows(c), :], core)
    for a in (0, 1):
        mine = acts[a].at[:, cols(xh)]
        send(("zn", "own", a), mine, tok.at[2, xh, c, xl, a], zn)
        send(("zp", "own", a), mine, tok.at[1, xh, c, xl, a], zp)

    def T1(a):
        for name, _, _, sxh, sxl in near:
            arrive("x0", name, a)
            block = tok.at[0, sxh, c, sxl, a]
            send(("c0", name, a), block, block, core)
            send(("zn", name, a), block, tok.at[2, sxh, c, sxl, a], zn)
            send(("zp", name, a), block, tok.at[1, sxh, c, sxl, a], zp)

    def T2(_):
        for way in ("zn", "zp"):
            for name in ("own", "xlp", "diag", "x2"):
                for a in (0, 1):
                    arrive(way, name, a)
        send(("zf", 0), tok.at[2, 0, c], tok.at[3, 0, c], zn)
        send(("zf", 1), tok.at[1, 1, c], tok.at[3, 1, c], zp)
        for k in (1, 2):
            send(("ck", k), tok.at[k, :, c], tok.at[k, :, c], core)

    def T3(_):
        for h in (0, 1):
            arrive("zf", h)
            send(("ck3", h), tok.at[3, h, c], tok.at[3, h, c], core)

    def project(k, a):
        left = tok[k, :, :, :, a // 2].reshape(chunk, feats)
        pp[k, :, :, a] = jnp.dot(left, w[a, :, :p_cols], preferred_element_type=F32).astype(BF16).reshape(4, 2, rows, p_cols)
        pq[k, :, :, a] = jnp.dot(left, w[a, :, p_cols:], preferred_element_type=F32).astype(BF16).reshape(4, 2, rows, q_cols)

    def groups(k):
        return ((0, 2), (2, 3)) if k == 0 else ((0, 3),)

    def F(k, g=0):
        first, last = groups(k)[g]
        if k == 0:
            local[g].wait()
            for name in ("own", "xlp", "diag", "x2"):
                arrive("c0", name, g)
            for a in range(first, last):
                local[2 + a].wait()
                arrive("w", a)
        elif k == 3:
            arrive("ck3", 0)
            arrive("ck3", 1)
        else:
            arrive("ck", k)

        @pl.loop(first, last)
        def _(a):
            project(k, a)

        part = slice(first, last)
        send(("s1", k, 0, g), pp.at[k, yo, 0, part], r1p.at[k, 0, part], ynd)
        send(("s1", k, 1, g), pp.at[k, yo, 1, part], r1p.at[k, 1, part], ypd)
        for j, t in enumerate((yo, yn, yp, y)):
            send(("qx", k, j, g), pq.at[k, t, oxh, part], rxq.at[k, t, part], x2)
        send(("s2i", k, 0, g), pp.at[k, yn, 1, part], r2p.at[k, 0, 1, part], ynd)
        send(("s2i", k, 1, g), pp.at[k, yp, 0, part], r2p.at[k, 1, 0, part], ypd)

    def arrive_groups(k, *name):
        for g in range(len(groups(k))):
            arrive(*name, g)

    def add(ref, *others):
        total = ref[...].astype(F32)
        for other in others:
            total += other[...].astype(F32)
        return total

    def A1(k):
        for way, t, device in ((0, yn, ynd), (1, yp, ypd)):
            arrive_groups(k, "s1", k, way)
            ref = pp.at[k, t, way]
            ref[...] = add(ref, r1p.at[k, way]).astype(BF16)
            send(("s2", k, way), ref, r2p.at[k, way, way], device)

    def add_x(k, j, t):
        arrive_groups(k, "qx", k, j)
        ref = pq.at[k, t, xh]
        ref[...] = add(ref, rxq.at[k, t]).astype(BF16)
        return ref

    def B1a(k):
        ref = add_x(k, 0, yo)
        send(("t1", k, 0), ref.at[:, :hr], r1q.at[k, 0], ynd)
        send(("t1", k, 1), ref.at[:, hr:], r1q.at[k, 1], ypd)

    def B1b(k):
        ref = add_x(k, 1, yn)
        send(("t2", k, 0, 1), ref.at[:, hr:], r2q.at[k, 0, :, hr:], ynd)
        ref = add_x(k, 2, yp)
        send(("t2", k, 1, 0), ref.at[:, :hr], r2q.at[k, 1, :, :hr], ypd)

    def B2(k):
        for way, t, device in ((0, yn, ynd), (1, yp, ypd)):
            arrive("t1", k, way)
            part = slice(0, hr) if way == 0 else slice(hr, rows)
            ref = pq.at[k, t, xh, :, part]
            ref[...] = add(ref, r1q.at[k, way]).astype(BF16)
            send(("t2", k, way, way), ref, r2q.at[k, way, :, part], device)

    def A2(k):
        for way in (0, 1):
            arrive("s2", k, way)
            arrive_groups(k, "s2i", k, way)
        ref = pp.at[k, y, oxh]
        ref[...] = add(ref, r2p.at[k, 0, oxh], r2p.at[k, 1, oxh]).astype(BF16)
        send(("rx", k), ref, rxp.at[k], x2)

    def activate(sums, out):
        gate, up, hidden_grad = sums[0], sums[1], sums[2]
        sigma = jax.nn.sigmoid(gate)
        active = gate * sigma
        out[0] = (hidden_grad * up * sigma * (1.0 + gate * (1.0 - sigma))).astype(BF16)
        out[1] = (hidden_grad * active).astype(BF16)
        out[2] = (active * up).astype(BF16)

    def A3(k):
        arrive("rx", k)
        activate(add(pp.at[k, y, xh], r2p.at[k, 0, xh], r2p.at[k, 1, xh], rxp.at[k]), dp.at[k, y, xh])

    def A3x(k):
        ref = dp.at[k, y, xh]
        send(("dx", k), ref, ref, x2)

    def A3y(k):
        ref = dp.at[k, y, xh]
        send(("do", k, 0), ref, ref, ynd)
        send(("do", k, 1), ref, ref, ypd)

    def B3(k):
        arrive_groups(k, "qx", k, 3)
        for way in (0, 1):
            for h in (0, 1):
                arrive("t2", k, way, h)
        activate(add(pq.at[k, y, xh], rxq.at[k, y], r2q.at[k, 0], r2q.at[k, 1]), dq.at[k, y, xh])

    def B3y(k):
        ref = dq.at[k, y, xh]
        send(("eo", k, 0), ref, ref, ynd)
        send(("eo", k, 1), ref, ref, ypd)

    def B3x(k):
        ref = dq.at[k, y, xh]
        send(("ex", k, 0), ref, ref, x2)

    def A4(k):
        arrive("dx", k)
        ref = dp.at[k, y, oxh]
        send(("dt", k, 0), ref, ref, ynd)
        send(("dt", k, 1), ref, ref, ypd)

    def A5a(k):
        arrive("do", k, 0)
        ref = dp.at[k, yp, xh]
        send(("df", k, 0), ref, ref, ynd)

    def A5b(k):
        arrive("dt", k, 1)
        ref = dp.at[k, yn, oxh]
        send(("df", k, 1), ref, ref, ypd)

    def B4y(k):
        arrive("eo", k, 0)
        ref = dq.at[k, yp, xh, :, :hr]
        send(("ef", k, 0), ref, ref, ynd)
        arrive("eo", k, 1)
        ref = dq.at[k, yn, xh, :, hr:]
        send(("ef", k, 1), ref, ref, ypd)

    def B4x(k):
        for j, t in ((1, yp), (2, yn)):
            ref = dq.at[k, t, xh]
            send(("ex", k, j), ref, ref, x2)

    def B5(k):
        arrive("ef", k, 0)
        arrive("ef", k, 1)
        ref = dq.at[k, yo, xh]
        send(("ex", k, 3), ref, ref, x2)

    def TR(k):
        @pl.loop(0, 2)
        def _(a):
            ttr[a, k] = tok[k, :, :, :, a].reshape(chunk, feats).T

    def C(k):
        for name in (("df", k, 0), ("df", k, 1), ("dt", k, 0), ("do", k, 1), ("ex", k, 0), ("ex", k, 1), ("ex", k, 2), ("ex", k, 3)):
            arrive(*name)
        nt = (((1,), (1,)), ((), ()))

        @pl.loop(0, 2)
        def _(j):
            fr = pl.ds(pl.multiple_of(j * own_f, 128), own_f)
            total = jnp.zeros((chunk, own_f), F32)
            for a in (0, 1):
                left = dp[k, :, :, a].reshape(chunk, p_cols)
                total += lax.dot_general(left, w[a, fr, :p_cols], nt, preferred_element_type=F32)
                left = dq[k, :, :, a].reshape(chunk, q_cols)
                total += lax.dot_general(left, w[a, fr, p_cols:], nt, preferred_element_type=F32)
            ig[k, :, :, :, :, fr] = total.astype(BF16).reshape(2, 2, 2, rows, own_f)

        send(("igc", k), ig.at[k, :, oc], rigc.at[k], core)

    def gradient(k, a, part, first, last, remote=False):
        left = ttr[a // 2, k, part, :]
        for ref, lanes in ((dp, slice(0, p_cols)), (dq, slice(p_cols, half))):
            right = ref[k, :, :, a].reshape(chunk, ref.shape[-1])
            value = jnp.dot(left, right, preferred_element_type=F32)
            if not first:
                value += acc[a, part, lanes]
            if last:
                if remote:
                    go[a, :, lanes] = value.astype(BF16)
                else:
                    lo = lanes.start
                    outs[a][:, pl.ds(pl.multiple_of(c * half + lo, 128), lanes.stop - lo)] = value.astype(BF16)
            else:
                acc[a, part, lanes] = value

    def G(k):
        TR(k)
        first, last = k == 1, k == 0
        if not last:
            @pl.loop(0, 6)
            def _(i):
                gradient(k, i // 2, pl.ds(pl.multiple_of((i % 2) * own_f, 128), own_f), first, last)
        else:
            for h, remote in ((oc, True), (c, False)):
                for a in range(3):
                    gradient(k, a, frows(h), first, last, remote)
                    if remote:
                        send(("go", a), go.at[a], outs[a].at[:, hcols(c)], core)

    def both(k, h):
        return ig[k, h, c].astype(F32) + rigc[k, h].astype(F32)

    def I3(_):
        arrive("igc", 3)
        for h in (0, 1):
            ref = ig.at[3, h, c]
            ref[...] = both(3, h).astype(BF16)
            send(("z1", h), ref, rz1.at[h], zn if h == 0 else zp)

    def I12(_):
        for k, device, way in ((1, zn, 0), (2, zp, 1)):
            arrive("igc", k)
            h = 1 - way
            ref = ig.at[k, h, c]
            ref[...] = both(k, h).astype(BF16)
            send(("z2", way, h), ref, rz2.at[way, h], device)

    def I12b(_):
        for k, device, way in ((1, zn, 0), (2, zp, 1)):
            arrive("z1", way)
            ref = ig.at[k, way, c]
            ref[...] = (both(k, way) + rz1[way].astype(F32)).astype(BF16)
            send(("z2", way, way), ref, rz2.at[way, way], device)

    def I0(_):
        arrive("igc", 0)
        for h in (0, 1):
            for way in (0, 1):
                arrive("z2", way, h)
            ig[0, h, c] = (both(0, h) + rz2[0, h].astype(F32) + rz2[1, h].astype(F32)).astype(BF16)
        send(("ix", 0), ig.at[0, xh, c, oxl], rix.at[0], xlp)
        send(("ix", 1), ig.at[0, oxh, c, oxl], rix.at[1], diag)
        send(("ix", 2), ig.at[0, oxh, c, xl], rix.at[2], x2)

    def I0f(_):
        for j in range(3):
            arrive("ix", j)
        ig_out[:, cols(xh)] = (ig[0, xh, c, xl].astype(F32) + rix[0].astype(F32)).astype(BF16)
        ig_out[:, cols(oxh)] = (rix[1].astype(F32) + rix[2].astype(F32)).astype(BF16)

    steps = dict(
        T1=T1, T2=T2, T3=T3, F=F, A1=A1, B1a=B1a, B1b=B1b, B2=B2, A2=A2, A3=A3, A3x=A3x, A3y=A3y, B3=B3, B3x=B3x,
        B3y=B3y, A4=A4, A5a=A5a, A5b=A5b, B4x=B4x, B4y=B4y, B5=B5, C=C, G=G, I3=I3, I12=I12, I12b=I12b, I0=I0, I0f=I0f,
    )
    for step, *k in ORDER:
        steps[step](*k)
    for a in range(3):
        arrive("go", a)
    for cp in all_sends:
        cp.wait_send()
    assert not arrivals, "left over"


def on_device(tokens, out_grad, gate_weight, up_weight, down_weight):
    rows, model = tokens.shape
    own_f, hidden = gate_weight.shape
    feats, half = 2 * own_f, hidden // 2
    q_cols = (half // 128 * 3 // 7) * 128
    p_cols = half - q_cols
    hr = rows // 2
    vmem = lambda *shape: pltpu.VMEM(shape, BF16)
    any_spec = pl.BlockSpec(memory_space=pl.ANY)
    out_shapes = [tokens, gate_weight, up_weight, down_weight]
    return pl.pallas_call(
        kernel,
        out_shape=[pltpu.VMEM(o.shape, BF16) for o in out_shapes],
        in_specs=[any_spec] * 5,
        out_specs=[pl.BlockSpec(memory_space=pltpu.VMEM)] * 4,
        scratch_shapes=[
            vmem(3, feats, half),
            vmem(4, 2, 2, 2, 2, rows, feats),
            vmem(2, 4, feats, 8 * rows),
            vmem(4, 4, 2, 3, rows, p_cols),
            vmem(4, 4, 2, 3, rows, q_cols),
            vmem(4, 2, 3, rows, p_cols),
            vmem(4, 2, 3, hr, q_cols),
            vmem(4, 2, 2, 3, rows, p_cols),
            vmem(4, 2, 3, rows, q_cols),
            vmem(4, 3, rows, p_cols),
            vmem(4, 4, 3, rows, q_cols),
            vmem(4, 4, 2, 3, rows, p_cols),
            vmem(4, 4, 2, 3, rows, q_cols),
            pltpu.VMEM((3, feats, half), F32),
            vmem(3, own_f, half),
            vmem(4, 2, 2, 2, rows, feats),
            vmem(4, 2, 2, rows, feats),
            vmem(2, 2, rows, feats),
            vmem(2, 2, 2, rows, feats),
            vmem(3, rows, feats),
            pltpu.SemaphoreType.DMA((N_SEM,)),
            pltpu.SemaphoreType.DMA((N_SEM,)),
            pltpu.SemaphoreType.DMA((16,)),
        ],
        compiler_params=pltpu.CompilerParams(
            collective_id=0, has_side_effects=True, vmem_limit_bytes=52 * 2**20
        ),
        cost_estimate=pl.CostEstimate(flops=15 * 10**9, bytes_accessed=12 * 2**20, transcendentals=10**6),
    )(tokens, out_grad, gate_weight, up_weight, down_weight)


def solution(mesh):
    in_specs = (
        P(("wt", "inp"), "out"),
        P(("wt", "inp"), "out"),
        P(("out", "wt"), "inp"),
        P(("out", "wt"), "inp"),
        P(("out", "wt"), "inp"),
    )
    out_specs = (
        P(("wt", "inp"), "out"),
        P(("out", "wt"), "inp"),
        P(("out", "wt"), "inp"),
        P(("out", "wt"), "inp"),
    )
    return jax.shard_map(
        on_device, mesh=mesh, in_specs=in_specs, out_specs=out_specs, check_vma=False
    )
```

```python
import functools

import jax
import jax.numpy as jnp
from jax import lax
from jax.experimental import pallas as pl
from jax.experimental.pallas import tpu as pltpu
from jax.sharding import PartitionSpec as P

BF16 = jnp.bfloat16
F32 = jnp.float32
MESH = pl.DeviceIdType.MESH
N_SEM = 240
PIECES = 4

ORDER = (
    ("R", 0), ("Z", 0), ("F", 0, 0), ("R", 1), ("F", 0, 1), ("Z", 1), ("F", 0, 2), ("T2", 0), ("A1", 0),
    ("F", 2, 0), ("T2", 1), ("F", 1, 0), ("F", 1, 1), ("F", 2, 1), ("T3", 0), ("B1a", 0), ("A1", 1), ("F", 3),
    ("A2", 1), ("A1", 2), ("A1", 3), ("B1a", 1), ("B1a", 3), ("B1b", 1), ("B1b", 3), ("A2", 2), ("A2", 3),
    ("B1a", 2), ("B2", 1), ("A3", 1), ("A3y", 1), ("A3x", 1), ("A3", 2), ("B1b", 2), ("B3", 1), ("B2", 3),
    ("B3y", 1), ("A3x", 2), ("B1b", 0), ("B2", 2), ("A2", 0), ("A3", 3), ("B3", 3), ("B3y", 3), ("A4", 1),
    ("A3x", 3), ("B4y", 1), ("B4x", 1), ("B3x", 1), ("B2", 0), ("B4y", 3), ("B3x", 3), ("A3y", 2), ("A5b", 1),
    ("B3", 2), ("B3y", 2), ("B3x", 2), ("A5a", 1), ("A3y", 3), ("B5", 1), ("B4x", 3), ("B5", 3), ("A3", 0),
    ("A3x", 0), ("A4", 3), ("A4", 2), ("B4y", 2), ("G", 1), ("C", 1, 0), ("B4x", 2), ("A5b", 3), ("A5a", 3),
    ("B3", 0), ("A5b", 2), ("A5a", 2), ("B5", 2), ("B3y", 0), ("A3y", 0), ("C", 3, 0), ("C", 3, 1), ("A4", 0),
    ("C", 1, 1), ("I3", 0), ("B3x", 0), ("C", 2, 0), ("B4y", 0), ("C", 2, 1), ("B4x", 0), ("I12", 0), ("A5a", 0),
    ("G", 2), ("A5b", 0), ("B5", 0), ("I12b", 0), ("G", 3), ("C", 0, 0), ("C", 0, 1), ("I0", 0), ("Gr", 0),
    ("Gl", 0), ("I0", 1), ("Gr", 1), ("Gr", 2), ("Gl", 1), ("Gl", 2), ("I0f", 0),
)


def kernel(
    tok_in, og_in, wg_in, wu_in, wd_in, ig_out, gg_out, ug_out, dg_out,
    w, tok, ttr, pp, pq, r1p, r1q, r2p, r2q, rxp, rxq, dp, dq, acc, go, ig, rigc, rz1, rz2, rix,
    ssem, rsem, lsem,
):
    inp, wt, y = lax.axis_index("inp"), lax.axis_index("wt"), lax.axis_index("out")
    xl, z, xh, c = inp // 4, inp % 4, wt // 2, wt % 2
    yn, yp, yo = (y + 1) % 4, (y + 3) % 4, (y + 2) % 4
    oxh, oxl, oc = 1 - xh, 1 - xl, 1 - c
    core = {"wt": xh * 2 + oc}
    x2 = {"wt": oxh * 2 + c}
    xlp = {"inp": oxl * 4 + z}
    diag = {"inp": oxl * 4 + z, "wt": oxh * 2 + c}
    zn, zp = {"inp": xl * 4 + (z + 1) % 4}, {"inp": xl * 4 + (z + 3) % 4}
    ynd, ypd = {"out": yn}, {"out": yp}
    feats, half = w.shape[1], w.shape[2]
    own_f = feats // 2
    p_cols, q_cols = pp.shape[-1], pq.shape[-1]
    rows = tok.shape[-2]
    chunk = 8 * rows
    hr = rows // 2
    cols = lambda h: pl.ds(pl.multiple_of(h * feats, 128), feats)
    hcols = lambda h: pl.ds(pl.multiple_of(h * half, 128), half)
    frows = lambda h: pl.ds(pl.multiple_of(h * own_f, 16), own_f)

    arrivals, all_sends, ready = {}, [], []

    def send(name, src, dst, device):
        i = len(all_sends)
        assert i < N_SEM
        cp = pltpu.make_async_remote_copy(
            src_ref=src, dst_ref=dst, send_sem=ssem.at[i], recv_sem=rsem.at[i], device_id=device, device_id_type=MESH
        )
        cp.start()
        all_sends.append(cp)
        arrivals[name] = cp

    def arrive(*name):
        arrivals.pop(name).wait_recv()

    local = []

    def bring(src, dst):
        cp = pltpu.make_async_copy(src, dst, lsem.at[len(local)])
        cp.start()
        local.append(cp)

    acts = (tok_in, og_in)
    outs = (gg_out, ug_out, dg_out)
    weights = (wg_in, wu_in, wd_in)
    for a in (0, 1):
        bring(acts[a].at[:, cols(xh)], tok.at[0, xh, c, xl, a])
    for a in range(3):
        bring(weights[a].at[:, hcols(c)], w.at[a, frows(c), :])

    barrier = pltpu.get_barrier_semaphore()
    for device in (core, x2, xlp, diag, zn, zp, ynd, ypd):
        pl.semaphore_signal(barrier, inc=1, device_id=device, device_id_type=MESH)
    pl.semaphore_wait(barrier, 8)

    near = (("x2", x2, oxh, oxh, xl), ("xlp", xlp, xh, xh, oxl), ("diag", diag, oxh, oxh, oxl))
    for a in (0, 1):
        for name, device, h, _, _ in near:
            send(("x0", name, a), acts[a].at[:, cols(h)], tok.at[0, xh, c, xl, a], device)
    for a in (0, 1):
        mine = acts[a].at[:, cols(xh)]
        send(("c0", "own", a), mine, tok.at[0, xh, c, xl, a], core)
    for a in range(3):
        send(("w", a), weights[a].at[:, hcols(oc)], w.at[a, frows(c), :], core)
    for a in (0, 1):
        mine = acts[a].at[:, cols(xh)]
        send(("zn", "own", a), mine, tok.at[2, xh, c, xl, a], zn)
        send(("zp", "own", a), mine, tok.at[1, xh, c, xl, a], zp)

    def R(a):
        for name, _, _, sxh, sxl in near:
            arrive("x0", name, a)
            block = tok.at[0, sxh, c, sxl, a]
            send(("c0", name, a), block, block, core)

    def Z(a):
        for name, _, _, sxh, sxl in near:
            block = tok.at[0, sxh, c, sxl, a]
            send(("zn", name, a), block, tok.at[2, sxh, c, sxl, a], zn)
            send(("zp", name, a), block, tok.at[1, sxh, c, sxl, a], zp)

    def T2(a):
        for way in ("zn", "zp"):
            for name in ("own", "xlp", "diag", "x2"):
                arrive(way, name, a)
        send(("zf", 0, a), tok.at[2, 0, c, :, a], tok.at[3, 0, c, :, a], zn)
        send(("zf", 1, a), tok.at[1, 1, c, :, a], tok.at[3, 1, c, :, a], zp)
        for k in (1, 2):
            send(("ck", k, a), tok.at[k, :, c, :, a], tok.at[k, :, c, :, a], core)

    def T3(_):
        for h in (0, 1):
            for a in (0, 1):
                arrive("zf", h, a)
            send(("ck3", h), tok.at[3, h, c], tok.at[3, h, c], core)

    def project(k, a):
        left = tok[k, :, :, :, a // 2].reshape(chunk, feats)
        pp[k, :, :, a] = jnp.dot(left, w[a, :, :p_cols], preferred_element_type=F32).astype(BF16).reshape(4, 2, rows, p_cols)
        pq[k, :, :, a] = jnp.dot(left, w[a, :, p_cols:], preferred_element_type=F32).astype(BF16).reshape(4, 2, rows, q_cols)

    def groups(k):
        return (((0, 1), (1, 2), (2, 3)), ((0, 2), (2, 3)), ((0, 2), (2, 3)), ((0, 3),))[k]

    def F(k, g=0):
        first, last = groups(k)[g]
        new = [a for a in (0, 1) if first <= 2 * a < last]
        for a in new if k < 3 else ():
            if k == 0:
                local[a].wait()
                for name in ("own", "xlp", "diag", "x2"):
                    arrive("c0", name, a)
            else:
                arrive("ck", k, a)
        if k == 0:
            for a in range(first, last):
                local[2 + a].wait()
                arrive("w", a)
        if k == 3:
            arrive("ck3", 0)
            arrive("ck3", 1)

        @pl.loop(first, last)
        def _(a):
            project(k, a)

        part = slice(first, last)
        send(("s1", k, 0, g), pp.at[k, yo, 0, part], r1p.at[k, 0, part], ynd)
        send(("s1", k, 1, g), pp.at[k, yo, 1, part], r1p.at[k, 1, part], ypd)
        for j, t in enumerate((yo, yn, yp, y)):
            send(("qx", k, j, g), pq.at[k, t, oxh, part], rxq.at[k, t, part], x2)
        send(("s2i", k, 0, g), pp.at[k, yn, 1, part], r2p.at[k, 0, 1, part], ynd)
        send(("s2i", k, 1, g), pp.at[k, yp, 0, part], r2p.at[k, 1, 0, part], ypd)

    def arrive_groups(k, *name):
        for g in range(len(groups(k))):
            arrive(*name, g)

    def add(ref, *others):
        total = ref[...].astype(F32)
        for other in others:
            total += other[...].astype(F32)
        return total

    def A1(k):
        for way, t, device in ((0, yn, ynd), (1, yp, ypd)):
            arrive_groups(k, "s1", k, way)
            ref = pp.at[k, t, way]
            ref[...] = add(ref, r1p.at[k, way]).astype(BF16)
            send(("s2", k, way), ref, r2p.at[k, way, way], device)

    def add_x(k, j, t):
        arrive_groups(k, "qx", k, j)
        ref = pq.at[k, t, xh]
        ref[...] = add(ref, rxq.at[k, t]).astype(BF16)
        return ref

    def B1a(k):
        ref = add_x(k, 0, yo)
        send(("t1", k, 0), ref.at[:, :hr], r1q.at[k, 0], ynd)
        send(("t1", k, 1), ref.at[:, hr:], r1q.at[k, 1], ypd)

    def B1b(k):
        ref = add_x(k, 1, yn)
        send(("t2", k, 0, 1), ref.at[:, hr:], r2q.at[k, 0, :, hr:], ynd)
        ref = add_x(k, 2, yp)
        send(("t2", k, 1, 0), ref.at[:, :hr], r2q.at[k, 1, :, :hr], ypd)

    def B2(k):
        for way, t, device in ((0, yn, ynd), (1, yp, ypd)):
            arrive("t1", k, way)
            part = slice(0, hr) if way == 0 else slice(hr, rows)
            ref = pq.at[k, t, xh, :, part]
            ref[...] = add(ref, r1q.at[k, way]).astype(BF16)
            send(("t2", k, way, way), ref, r2q.at[k, way, :, part], device)

    def A2(k):
        for way in (0, 1):
            arrive("s2", k, way)
            arrive_groups(k, "s2i", k, way)
        ref = pp.at[k, y, oxh]
        ref[...] = add(ref, r2p.at[k, 0, oxh], r2p.at[k, 1, oxh]).astype(BF16)
        send(("rx", k), ref, rxp.at[k], x2)

    def activate(sums, out):
        gate, up, hidden_grad = sums[0], sums[1], sums[2]
        sigma = jax.nn.sigmoid(gate)
        active = gate * sigma
        out[0] = (hidden_grad * up * sigma * (1.0 + gate * (1.0 - sigma))).astype(BF16)
        out[1] = (hidden_grad * active).astype(BF16)
        out[2] = (active * up).astype(BF16)

    def A3(k):
        arrive("rx", k)
        activate(add(pp.at[k, y, xh], r2p.at[k, 0, xh], r2p.at[k, 1, xh], rxp.at[k]), dp.at[k, y, xh])

    def A3x(k):
        ref = dp.at[k, y, xh]
        send(("dx", k), ref, ref, x2)

    def A3y(k):
        ref = dp.at[k, y, xh]
        send(("do", k, 0), ref, ref, ynd)
        send(("do", k, 1), ref, ref, ypd)

    def B3(k):
        arrive_groups(k, "qx", k, 3)
        for way in (0, 1):
            for h in (0, 1):
                arrive("t2", k, way, h)
        activate(add(pq.at[k, y, xh], rxq.at[k, y], r2q.at[k, 0], r2q.at[k, 1]), dq.at[k, y, xh])

    def B3y(k):
        ref = dq.at[k, y, xh]
        send(("eo", k, 0), ref, ref, ynd)
        send(("eo", k, 1), ref, ref, ypd)

    def B3x(k):
        ref = dq.at[k, y, xh]
        send(("ex", k, 0), ref, ref, x2)

    def A4(k):
        arrive("dx", k)
        ref = dp.at[k, y, oxh]
        send(("dt", k, 0), ref, ref, ynd)
        send(("dt", k, 1), ref, ref, ypd)

    def A5a(k):
        arrive("do", k, 0)
        ref = dp.at[k, yp, xh]
        send(("df", k, 0), ref, ref, ynd)

    def A5b(k):
        arrive("dt", k, 1)
        ref = dp.at[k, yn, oxh]
        send(("df", k, 1), ref, ref, ypd)

    def B4y(k):
        arrive("eo", k, 0)
        ref = dq.at[k, yp, xh, :, :hr]
        send(("ef", k, 0), ref, ref, ynd)
        arrive("eo", k, 1)
        ref = dq.at[k, yn, xh, :, hr:]
        send(("ef", k, 1), ref, ref, ypd)

    def B4x(k):
        for j, t in ((1, yp), (2, yn)):
            ref = dq.at[k, t, xh]
            send(("ex", k, j), ref, ref, x2)

    def B5(k):
        arrive("ef", k, 0)
        arrive("ef", k, 1)
        ref = dq.at[k, yo, xh]
        send(("ex", k, 3), ref, ref, x2)

    def TR(k):
        @pl.loop(0, 2)
        def _(a):
            ttr[a, k] = tok[k, :, :, :, a].reshape(chunk, feats).T

    def whole(k):
        for name in [("df", k, 0), ("df", k, 1), ("dt", k, 0), ("do", k, 1)] + [("ex", k, n) for n in range(4)]:
            if name in arrivals:
                arrive(*name)

    def C(k, j):
        whole(k)
        nt = (((1,), (1,)), ((), ()))
        fr = slice(j * own_f, (j + 1) * own_f)
        total = jnp.zeros((chunk, own_f), F32)
        for a in (0, 1):
            left = dp[k, :, :, a].reshape(chunk, p_cols)
            total += lax.dot_general(left, w[a, fr, :p_cols], nt, preferred_element_type=F32)
            left = dq[k, :, :, a].reshape(chunk, q_cols)
            total += lax.dot_general(left, w[a, fr, p_cols:], nt, preferred_element_type=F32)
        ig[k, :, :, :, :, fr] = total.astype(BF16).reshape(2, 2, 2, rows, own_f)
        send(("igc", k, j), ig.at[k, :, oc, :, :, fr], rigc.at[k, :, :, :, fr], core)

    def gradient(k, a, part, first, last, remote=False):
        left = ttr[a // 2, k, part, :]
        for ref, lanes in ((dp, slice(0, p_cols)), (dq, slice(p_cols, half))):
            right = ref[k, :, :, a].reshape(chunk, ref.shape[-1])
            value = jnp.dot(left, right, preferred_element_type=F32)
            if not first:
                value += acc[a, part, lanes]
            if last:
                if remote:
                    go[a, :, lanes] = value.astype(BF16)
                else:
                    lo = lanes.start
                    outs[a][:, pl.ds(pl.multiple_of(c * half + lo, 128), lanes.stop - lo)] = value.astype(BF16)
            else:
                acc[a, part, lanes] = value

    def G(k):
        whole(k)
        TR(k)

        @pl.loop(0, 6)
        def _(i):
            gradient(k, i // 2, pl.ds(pl.multiple_of((i % 2) * own_f, 128), own_f), k == 1, False)

    def last_chunk():
        whole(0)
        if not ready:
            ready.append(0)
            TR(0)

    def Gr(a):
        last_chunk()
        gradient(0, a, frows(oc), False, True, True)
        send(("go", a), go.at[a], outs[a].at[:, hcols(c)], core)

    def Gl(a):
        last_chunk()
        gradient(0, a, frows(c), False, True)

    def both(k, h):
        return ig[k, h, c].astype(F32) + rigc[k, h].astype(F32)

    def I3(_):
        arrive("igc", 3, 0)
        arrive("igc", 3, 1)
        for h in (0, 1):
            ref = ig.at[3, h, c]
            ref[...] = both(3, h).astype(BF16)
            send(("z1", h), ref, rz1.at[h], zn if h == 0 else zp)

    def I12(_):
        for k, device, way in ((1, zn, 0), (2, zp, 1)):
            arrive("igc", k, 0)
            arrive("igc", k, 1)
            h = 1 - way
            ref = ig.at[k, h, c]
            ref[...] = both(k, h).astype(BF16)
            send(("z2", way, h), ref, rz2.at[way, h], device)

    def I12b(_):
        for k, device, way in ((1, zn, 0), (2, zp, 1)):
            arrive("z1", way)
            ref = ig.at[k, way, c]
            ref[...] = (both(k, way) + rz1[way].astype(F32)).astype(BF16)
            send(("z2", way, way), ref, rz2.at[way, way], device)

    def I0(j):
        arrive("igc", 0, j)
        fr = slice(j * own_f, (j + 1) * own_f)
        for h in (0, 1):
            if j == 0:
                for way in (0, 1):
                    arrive("z2", way, h)
            total = ig[0, h, c, :, :, fr].astype(F32) + rigc[0, h, :, :, fr].astype(F32)
            total += rz2[0, h, :, :, fr].astype(F32) + rz2[1, h, :, :, fr].astype(F32)
            ig[0, h, c, :, :, fr] = total.astype(BF16)
        send(("ix", 2, j), ig.at[0, oxh, c, xl, :, fr], rix.at[2, :, fr], x2)
        send(("ix", 0, j), ig.at[0, xh, c, oxl, :, fr], rix.at[0, :, fr], xlp)
        send(("ix", 1, j), ig.at[0, oxh, c, oxl, :, fr], rix.at[1, :, fr], diag)

    def I0f(_):
        for j in (0, 1):
            for n in range(3):
                arrive("ix", n, j)
        ig_out[:, cols(xh)] = (ig[0, xh, c, xl].astype(F32) + rix[0].astype(F32)).astype(BF16)
        ig_out[:, cols(oxh)] = (rix[1].astype(F32) + rix[2].astype(F32)).astype(BF16)

    steps = dict(
        R=R, Z=Z, T2=T2, T3=T3, F=F, A1=A1, B1a=B1a, B1b=B1b, B2=B2, A2=A2, A3=A3, A3x=A3x, A3y=A3y, B3=B3, B3x=B3x,
        B3y=B3y, A4=A4, A5a=A5a, A5b=A5b, B4x=B4x, B4y=B4y, B5=B5, C=C, G=G, Gr=Gr, Gl=Gl, I3=I3, I12=I12, I12b=I12b,
        I0=I0, I0f=I0f,
    )
    for step, *k in ORDER:
        steps[step](*k)
    for a in range(3):
        arrive("go", a)
    for cp in all_sends:
        cp.wait_send()
    assert not arrivals, "left over"


def write_out(a, b, c, d, ao, bo, co, do, sem):
    copies = []
    for i, (src, dst) in enumerate(((b, bo), (c, co), (d, do), (a, ao))):
        n = PIECES if src.shape[0] >= 16 * PIECES else 1
        step = src.shape[0] // n
        for j in range(n):
            part = pl.ds(j * step, step)
            cp = pltpu.make_async_copy(src.at[part], dst.at[part], sem.at[i, j])
            cp.start()
            copies.append(cp)
    for cp in copies:
        cp.wait()


def on_device(tokens, out_grad, gate_weight, up_weight, down_weight):
    rows, model = tokens.shape
    own_f, hidden = gate_weight.shape
    feats, half = 2 * own_f, hidden // 2
    q_cols = (half // 128 * 3 // 7) * 128
    p_cols = half - q_cols
    hr = rows // 2
    vmem = lambda *shape: pltpu.VMEM(shape, BF16)
    any_spec = pl.BlockSpec(memory_space=pl.ANY)
    out_shapes = [tokens, gate_weight, up_weight, down_weight]
    grads = pl.pallas_call(
        kernel,
        out_shape=[pltpu.VMEM(o.shape, BF16) for o in out_shapes],
        in_specs=[any_spec] * 5,
        out_specs=[pl.BlockSpec(memory_space=pltpu.VMEM)] * 4,
        scratch_shapes=[
            vmem(3, feats, half),
            vmem(4, 2, 2, 2, 2, rows, feats),
            vmem(2, 4, feats, 8 * rows),
            vmem(4, 4, 2, 3, rows, p_cols),
            vmem(4, 4, 2, 3, rows, q_cols),
            vmem(4, 2, 3, rows, p_cols),
            vmem(4, 2, 3, hr, q_cols),
            vmem(4, 2, 2, 3, rows, p_cols),
            vmem(4, 2, 3, rows, q_cols),
            vmem(4, 3, rows, p_cols),
            vmem(4, 4, 3, rows, q_cols),
            vmem(4, 4, 2, 3, rows, p_cols),
            vmem(4, 4, 2, 3, rows, q_cols),
            pltpu.VMEM((3, feats, half), F32),
            vmem(3, own_f, half),
            vmem(4, 2, 2, 2, rows, feats),
            vmem(4, 2, 2, rows, feats),
            vmem(2, 2, rows, feats),
            vmem(2, 2, 2, rows, feats),
            vmem(3, rows, feats),
            pltpu.SemaphoreType.DMA((N_SEM,)),
            pltpu.SemaphoreType.DMA((N_SEM,)),
            pltpu.SemaphoreType.DMA((16,)),
        ],
        compiler_params=pltpu.CompilerParams(
            collective_id=0, has_side_effects=True, vmem_limit_bytes=52 * 2**20
        ),
        cost_estimate=pl.CostEstimate(flops=15 * 10**9, bytes_accessed=12 * 2**20, transcendentals=10**6),
    )(tokens, out_grad, gate_weight, up_weight, down_weight)
    return pl.pallas_call(
        write_out,
        out_shape=[jax.ShapeDtypeStruct(o.shape, BF16) for o in out_shapes],
        in_specs=[any_spec] * 4,
        out_specs=[any_spec] * 4,
        scratch_shapes=[pltpu.SemaphoreType.DMA((4, PIECES))],
        compiler_params=pltpu.CompilerParams(vmem_limit_bytes=2 * 2**20),
        cost_estimate=pl.CostEstimate(flops=0, bytes_accessed=12 * 2**20, transcendentals=0),
    )(*grads)


def solution(mesh):
    in_specs = (
        P(("wt", "inp"), "out"),
        P(("wt", "inp"), "out"),
        P(("out", "wt"), "inp"),
        P(("out", "wt"), "inp"),
        P(("out", "wt"), "inp"),
    )
    out_specs = (
        P(("wt", "inp"), "out"),
        P(("out", "wt"), "inp"),
        P(("out", "wt"), "inp"),
        P(("out", "wt"), "inp"),
    )
    return jax.shard_map(
        on_device, mesh=mesh, in_specs=in_specs, out_specs=out_specs, check_vma=False
    )
```

```python
import functools

import jax
import jax.numpy as jnp
from jax import lax
from jax.experimental import pallas as pl
from jax.experimental.pallas import tpu as pltpu
from jax.sharding import PartitionSpec as P

BF16 = jnp.bfloat16
F32 = jnp.float32
MESH = pl.DeviceIdType.MESH
N_SEM = 272
PIECES = 4

ORDER = (
    ("R", 0), ("Z", 0), ("F", 0, 0), ("R", 1), ("F", 0, 1), ("Z", 1), ("F", 0, 2), ("T2", 0), ("A1", 0),
    ("F", 1, 0), ("B1a", 0), ("T2", 1), ("F", 1, 1), ("F", 2, 0), ("F", 2, 1), ("T3", 0), ("A1", 1), ("F", 3),
    ("B1a", 2), ("B1a", 1), ("B1b", 2), ("A1", 2), ("B1a", 3), ("A1", 3), ("A2", 1), ("B2", 2), ("B1b", 1),
    ("B1b", 0), ("A2", 0), ("A2", 2), ("B1b", 3), ("A3", 1), ("A2", 3), ("A3x", 1, 0), ("B2", 1), ("A3", 0),
    ("B2", 0), ("B2", 3), ("B3", 2), ("B3y", 2, 0), ("A3x", 0, 0), ("B3x", 2, 0), ("A3y", 1, 0), ("B3", 1),
    ("A3", 3), ("B3", 3), ("B3x", 3, 0), ("B3y", 1, 0), ("B3y", 3, 0), ("A3x", 3, 0), ("A4", 1, 0), ("A3", 2),
    ("A3x", 2, 0), ("B4y", 1, 0), ("A5a", 1, 0), ("B4y", 3, 0), ("B4x", 1, 0), ("A3y", 3, 0), ("B5", 1, 0),
    ("B3x", 1, 0), ("B4y", 2, 0), ("A5b", 1, 0), ("B3", 0), ("A4", 3, 0), ("A3y", 2, 0), ("B4x", 3, 0),
    ("A5a", 3, 0), ("B5", 3, 0), ("A4", 2, 0), ("C", 1, 0), ("B5", 2, 0), ("G", 1, 2), ("A5b", 3, 0), ("A5a", 2, 0),
    ("B4x", 2, 0), ("A3x", 0, 1), ("C", 1, 1), ("G", 1, 0), ("A5b", 2, 0), ("B3y", 0, 0), ("A3y", 0, 0),
    ("G", 1, 1), ("A4", 0, 0), ("C", 3, 0), ("C", 3, 1), ("G", 3, 2), ("I3", 0), ("C", 2, 0), ("C", 2, 1),
    ("B3y", 0, 1), ("B4y", 0, 0), ("B4x", 0, 0), ("A3y", 0, 1), ("A4", 0, 1), ("A5a", 0, 0), ("I12", 0),
    ("G", 2, 0), ("A5b", 0, 0), ("B3x", 0, 0), ("G", 3, 1), ("B5", 0, 0), ("I12b", 0), ("G", 3, 0), ("A5a", 0, 1),
    ("B4y", 0, 1), ("A5b", 0, 1), ("G", 2, 1), ("Gp", 0), ("B4x", 0, 1), ("CP", 0), ("B3x", 0, 1), ("C", 0, 0),
    ("C", 0, 1), ("B5", 0, 1), ("C", 0, 2), ("Gp", 1), ("I0", 0), ("C", 0, 3), ("I0", 1), ("I0", 2), ("Gr", 1),
    ("Gl", 0), ("I0", 3), ("G", 2, 2), ("Gr", 0), ("Gp", 2), ("Gr", 2), ("Gl", 2), ("Gl", 1), ("I0f", 0),
)


def kernel(
    tok_in, og_in, wg_in, wu_in, wd_in, ig_out, gg_out, ug_out, dg_out,
    w, tok, ttr, pp, pq, r1p, r1q, r2p, r2q, rxp, rxq, dp, dq, acc, go, ig, rigc, rz1, rz2, rix, igp,
    ssem, rsem, lsem,
):
    inp, wt, y = lax.axis_index("inp"), lax.axis_index("wt"), lax.axis_index("out")
    xl, z, xh, c = inp // 4, inp % 4, wt // 2, wt % 2
    yn, yp, yo = (y + 1) % 4, (y + 3) % 4, (y + 2) % 4
    oxh, oxl, oc = 1 - xh, 1 - xl, 1 - c
    core = {"wt": xh * 2 + oc}
    x2 = {"wt": oxh * 2 + c}
    xlp = {"inp": oxl * 4 + z}
    diag = {"inp": oxl * 4 + z, "wt": oxh * 2 + c}
    zn, zp = {"inp": xl * 4 + (z + 1) % 4}, {"inp": xl * 4 + (z + 3) % 4}
    ynd, ypd = {"out": yn}, {"out": yp}
    feats, half = w.shape[1], w.shape[2]
    own_f = feats // 2
    p_cols, q_cols = pp.shape[-1], pq.shape[-1]
    rows = tok.shape[-2]
    chunk = 8 * rows
    hr = rows // 2
    cols = lambda h: pl.ds(pl.multiple_of(h * feats, 128), feats)
    hcols = lambda h: pl.ds(pl.multiple_of(h * half, 128), half)
    frows = lambda h: pl.ds(pl.multiple_of(h * own_f, 16), own_f)

    arrivals, all_sends, ready = {}, [], []

    def send(name, src, dst, device):
        i = len(all_sends)
        assert i < N_SEM
        cp = pltpu.make_async_remote_copy(
            src_ref=src, dst_ref=dst, send_sem=ssem.at[i], recv_sem=rsem.at[i], device_id=device, device_id_type=MESH
        )
        cp.start()
        all_sends.append(cp)
        arrivals[name] = cp

    def arrive(*name):
        arrivals.pop(name).wait_recv()

    local = []

    def bring(src, dst):
        cp = pltpu.make_async_copy(src, dst, lsem.at[len(local)])
        cp.start()
        local.append(cp)

    acts = (tok_in, og_in)
    outs = (gg_out, ug_out, dg_out)
    weights = (wg_in, wu_in, wd_in)
    for a in (0, 1):
        bring(acts[a].at[:, cols(xh)], tok.at[0, xh, c, xl, a])
    for a in range(3):
        bring(weights[a].at[:, hcols(c)], w.at[a, frows(c), :])

    barrier = pltpu.get_barrier_semaphore()
    for device in (core, x2, xlp, diag, zn, zp, ynd, ypd):
        pl.semaphore_signal(barrier, inc=1, device_id=device, device_id_type=MESH)
    pl.semaphore_wait(barrier, 8)

    near = (("x2", x2, oxh, oxh, xl), ("xlp", xlp, xh, xh, oxl), ("diag", diag, oxh, oxh, oxl))
    for a in (0, 1):
        for name, device, h, _, _ in near:
            send(("x0", name, a), acts[a].at[:, cols(h)], tok.at[0, xh, c, xl, a], device)
    for a in (0, 1):
        mine = acts[a].at[:, cols(xh)]
        send(("c0", "own", a), mine, tok.at[0, xh, c, xl, a], core)
    for a in range(3):
        send(("w", a), weights[a].at[:, hcols(oc)], w.at[a, frows(c), :], core)
    for a in (0, 1):
        mine = acts[a].at[:, cols(xh)]
        send(("zn", "own", a), mine, tok.at[2, xh, c, xl, a], zn)
        send(("zp", "own", a), mine, tok.at[1, xh, c, xl, a], zp)

    def R(a):
        for name, _, _, sxh, sxl in near:
            arrive("x0", name, a)
            block = tok.at[0, sxh, c, sxl, a]
            send(("c0", name, a), block, block, core)

    def Z(a):
        for name, _, _, sxh, sxl in near:
            block = tok.at[0, sxh, c, sxl, a]
            send(("zn", name, a), block, tok.at[2, sxh, c, sxl, a], zn)
            send(("zp", name, a), block, tok.at[1, sxh, c, sxl, a], zp)

    def T2(a):
        for way in ("zn", "zp"):
            for name in ("own", "xlp", "diag", "x2"):
                arrive(way, name, a)
        send(("zf", 0, a), tok.at[2, 0, c, :, a], tok.at[3, 0, c, :, a], zn)
        send(("zf", 1, a), tok.at[1, 1, c, :, a], tok.at[3, 1, c, :, a], zp)
        for k in (1, 2):
            send(("ck", k, a), tok.at[k, :, c, :, a], tok.at[k, :, c, :, a], core)

    def T3(_):
        for h in (0, 1):
            for a in (0, 1):
                arrive("zf", h, a)
            send(("ck3", h), tok.at[3, h, c], tok.at[3, h, c], core)

    def project(k, a):
        left = tok[k, :, :, :, a // 2].reshape(chunk, feats)
        pp[k, :, :, a] = jnp.dot(left, w[a, :, :p_cols], preferred_element_type=F32).astype(BF16).reshape(4, 2, rows, p_cols)
        pq[k, :, :, a] = jnp.dot(left, w[a, :, p_cols:], preferred_element_type=F32).astype(BF16).reshape(4, 2, rows, q_cols)

    def groups(k):
        return (((0, 1), (1, 2), (2, 3)), ((0, 2), (2, 3)), ((0, 2), (2, 3)), ((0, 3),))[k]

    def F(k, g=0):
        first, last = groups(k)[g]
        new = [a for a in (0, 1) if first <= 2 * a < last]
        for a in new if k < 3 else ():
            if k == 0:
                local[a].wait()
                for name in ("own", "xlp", "diag", "x2"):
                    arrive("c0", name, a)
            else:
                arrive("ck", k, a)
        if k == 0:
            for a in range(first, last):
                local[2 + a].wait()
                arrive("w", a)
        if k == 3:
            arrive("ck3", 0)
            arrive("ck3", 1)

        @pl.loop(first, last)
        def _(a):
            project(k, a)

        part = slice(first, last)
        send(("s1", k, 0, g), pp.at[k, yo, 0, part], r1p.at[k, 0, part], ynd)
        send(("s1", k, 1, g), pp.at[k, yo, 1, part], r1p.at[k, 1, part], ypd)
        for j, t in enumerate((yo, yn, yp, y)):
            send(("qx", k, j, g), pq.at[k, t, oxh, part], rxq.at[k, t, part], x2)
        send(("s2i", k, 0, g), pp.at[k, yn, 1, part], r2p.at[k, 0, 1, part], ynd)
        send(("s2i", k, 1, g), pp.at[k, yp, 0, part], r2p.at[k, 1, 0, part], ypd)

    def arrive_groups(k, *name):
        for g in range(len(groups(k))):
            arrive(*name, g)

    def add(ref, *others):
        total = ref[...].astype(F32)
        for other in others:
            total += other[...].astype(F32)
        return total

    def A1(k):
        for way, t, device in ((0, yn, ynd), (1, yp, ypd)):
            arrive_groups(k, "s1", k, way)
            ref = pp.at[k, t, way]
            ref[...] = add(ref, r1p.at[k, way]).astype(BF16)
            send(("s2", k, way), ref, r2p.at[k, way, way], device)

    def add_x(k, j, t):
        arrive_groups(k, "qx", k, j)
        ref = pq.at[k, t, xh]
        ref[...] = add(ref, rxq.at[k, t]).astype(BF16)
        return ref

    def B1a(k):
        ref = add_x(k, 0, yo)
        send(("t1", k, 0), ref.at[:, :hr], r1q.at[k, 0], ynd)
        send(("t1", k, 1), ref.at[:, hr:], r1q.at[k, 1], ypd)

    def B1b(k):
        ref = add_x(k, 1, yn)
        send(("t2", k, 0, 1), ref.at[:, hr:], r2q.at[k, 0, :, hr:], ynd)
        ref = add_x(k, 2, yp)
        send(("t2", k, 1, 0), ref.at[:, :hr], r2q.at[k, 1, :, :hr], ypd)

    def B2(k):
        for way, t, device in ((0, yn, ynd), (1, yp, ypd)):
            arrive("t1", k, way)
            part = slice(0, hr) if way == 0 else slice(hr, rows)
            ref = pq.at[k, t, xh, :, part]
            ref[...] = add(ref, r1q.at[k, way]).astype(BF16)
            send(("t2", k, way, way), ref, r2q.at[k, way, :, part], device)

    def A2(k):
        for way in (0, 1):
            arrive("s2", k, way)
            arrive_groups(k, "s2i", k, way)
        ref = pp.at[k, y, oxh]
        ref[...] = add(ref, r2p.at[k, 0, oxh], r2p.at[k, 1, oxh]).astype(BF16)
        send(("rx", k), ref, rxp.at[k], x2)

    def activate(sums, out):
        gate, up, hidden_grad = sums[0], sums[1], sums[2]
        sigma = jax.nn.sigmoid(gate)
        active = gate * sigma
        out[0] = (hidden_grad * up * sigma * (1.0 + gate * (1.0 - sigma))).astype(BF16)
        out[1] = (hidden_grad * active).astype(BF16)
        out[2] = (active * up).astype(BF16)

    def A3(k):
        arrive("rx", k)
        activate(add(pp.at[k, y, xh], r2p.at[k, 0, xh], r2p.at[k, 1, xh], rxp.at[k]), dp.at[k, y, xh])

    def B3(k):
        arrive_groups(k, "qx", k, 3)
        for way in (0, 1):
            for h in (0, 1):
                arrive("t2", k, way, h)
        activate(add(pq.at[k, y, xh], rxq.at[k, y], r2q.at[k, 0], r2q.at[k, 1]), dq.at[k, y, xh])

    def late(k, g):
        return (slice(0, 2), slice(2, 3))[g] if k == 0 else slice(0, 3)

    def A3x(k, g):
        ref = dp.at[k, y, xh, late(k, g)]
        send(("dx", k, g), ref, ref, x2)

    def A3y(k, g):
        ref = dp.at[k, y, xh, late(k, g)]
        send(("do", k, 0, g), ref, ref, ynd)
        send(("do", k, 1, g), ref, ref, ypd)

    def B3y(k, g):
        ref = dq.at[k, y, xh, late(k, g)]
        send(("eo", k, 0, g), ref, ref, ynd)
        send(("eo", k, 1, g), ref, ref, ypd)

    def B3x(k, g):
        ref = dq.at[k, y, xh, late(k, g)]
        send(("ex", k, 0, g), ref, ref, x2)

    def A4(k, g):
        arrive("dx", k, g)
        ref = dp.at[k, y, oxh, late(k, g)]
        send(("dt", k, 0, g), ref, ref, ynd)
        send(("dt", k, 1, g), ref, ref, ypd)

    def A5a(k, g):
        arrive("do", k, 0, g)
        ref = dp.at[k, yp, xh, late(k, g)]
        send(("df", k, 0, g), ref, ref, ynd)

    def A5b(k, g):
        arrive("dt", k, 1, g)
        ref = dp.at[k, yn, oxh, late(k, g)]
        send(("df", k, 1, g), ref, ref, ypd)

    def B4y(k, g):
        arrive("eo", k, 0, g)
        ref = dq.at[k, yp, xh, late(k, g), :hr]
        send(("ef", k, 0, g), ref, ref, ynd)
        arrive("eo", k, 1, g)
        ref = dq.at[k, yn, xh, late(k, g), hr:]
        send(("ef", k, 1, g), ref, ref, ypd)

    def B4x(k, g):
        for j, t in ((1, yp), (2, yn)):
            ref = dq.at[k, t, xh, late(k, g)]
            send(("ex", k, j, g), ref, ref, x2)

    def B5(k, g):
        arrive("ef", k, 0, g)
        arrive("ef", k, 1, g)
        ref = dq.at[k, yo, xh, late(k, g)]
        send(("ex", k, 3, g), ref, ref, x2)

    def TR(k):
        @pl.loop(0, 2)
        def _(a):
            ttr[a, k] = tok[k, :, :, :, a].reshape(chunk, feats).T

    def whole_p(k, g=0):
        for name in (("df", k, 0, g), ("df", k, 1, g), ("dt", k, 0, g), ("do", k, 1, g)):
            if name in arrivals:
                arrive(*name)

    def whole(k, g=0):
        whole_p(k, g)
        for n in range(4):
            if ("ex", k, n, g) in arrivals:
                arrive("ex", k, n, g)

    def back(k, ref, fr, lanes):
        total = None
        for a in (0, 1):
            left = ref[k, :, :, a].reshape(chunk, ref.shape[-1])
            part = lax.dot_general(left, w[a, fr, lanes], (((1,), (1,)), ((), ())), preferred_element_type=F32)
            total = part if total is None else total + part
        return total

    def pieces(k):
        n = PIECES if k == 0 else 2
        return [slice(j * (feats // n), (j + 1) * (feats // n)) for j in range(n)]

    def CP(_):
        whole_p(0)
        for fr in pieces(1):
            igp[:, fr] = back(0, dp, fr, slice(0, p_cols))

    def C(k, j):
        whole(k)
        fr = pieces(k)[j]
        total = back(k, dq, fr, slice(p_cols, half))
        total += igp[:, fr] if k == 0 else back(k, dp, fr, slice(0, p_cols))
        ig[k, :, :, :, :, fr] = total.astype(BF16).reshape(2, 2, 2, rows, total.shape[-1])
        send(("igc", k, j), ig.at[k, :, oc, :, :, fr], rigc.at[k, :, :, :, fr], core)

    def gradient(k, a, part, first, last, remote=False, sets=(0, 1)):
        left = ttr[a // 2, k, part, :]
        for ref, lanes in [((dp, slice(0, p_cols)), (dq, slice(p_cols, half)))[n] for n in sets]:
            right = ref[k, :, :, a].reshape(chunk, ref.shape[-1])
            value = jnp.dot(left, right, preferred_element_type=F32)
            if not first:
                value += acc[a, part, lanes]
            if last:
                if remote:
                    go[a, :, lanes] = value.astype(BF16)
                else:
                    lo = lanes.start
                    outs[a][:, pl.ds(pl.multiple_of(c * half + lo, 128), lanes.stop - lo)] = value.astype(BF16)
            else:
                acc[a, part, lanes] = value

    def turned(k):
        if k not in ready:
            ready.append(k)
            TR(k)

    def G(k, a):
        whole(k)
        turned(k)

        @pl.loop(0, 2)
        def _(i):
            gradient(k, a, pl.ds(pl.multiple_of(i * own_f, 128), own_f), k == 1, False)

    def Gp(a):
        whole_p(0, a // 2)
        turned(0)
        gradient(0, a, frows(oc), False, True, True, (0,))
        gradient(0, a, frows(c), False, True, False, (0,))

    def Gr(a):
        whole(0, a // 2)
        gradient(0, a, frows(oc), False, True, True, (1,))
        send(("go", a), go.at[a], outs[a].at[:, hcols(c)], core)

    def Gl(a):
        whole(0, a // 2)
        gradient(0, a, frows(c), False, True, False, (1,))

    def both(k, h):
        return ig[k, h, c].astype(F32) + rigc[k, h].astype(F32)

    def I3(_):
        arrive("igc", 3, 0)
        arrive("igc", 3, 1)
        for h in (0, 1):
            ref = ig.at[3, h, c]
            ref[...] = both(3, h).astype(BF16)
            send(("z1", h), ref, rz1.at[h], zn if h == 0 else zp)

    def I12(_):
        for k, device, way in ((1, zn, 0), (2, zp, 1)):
            arrive("igc", k, 0)
            arrive("igc", k, 1)
            h = 1 - way
            ref = ig.at[k, h, c]
            ref[...] = both(k, h).astype(BF16)
            send(("z2", way, h), ref, rz2.at[way, h], device)

    def I12b(_):
        for k, device, way in ((1, zn, 0), (2, zp, 1)):
            arrive("z1", way)
            ref = ig.at[k, way, c]
            ref[...] = (both(k, way) + rz1[way].astype(F32)).astype(BF16)
            send(("z2", way, way), ref, rz2.at[way, way], device)

    def I0(j):
        arrive("igc", 0, j)
        fr = pieces(0)[j]
        for h in (0, 1):
            if j == 0:
                for way in (0, 1):
                    arrive("z2", way, h)
            total = ig[0, h, c, :, :, fr].astype(F32) + rigc[0, h, :, :, fr].astype(F32)
            total += rz2[0, h, :, :, fr].astype(F32) + rz2[1, h, :, :, fr].astype(F32)
            ig[0, h, c, :, :, fr] = total.astype(BF16)
        send(("ix", 2, j), ig.at[0, oxh, c, xl, :, fr], rix.at[2, :, fr], x2)
        send(("ix", 0, j), ig.at[0, xh, c, oxl, :, fr], rix.at[0, :, fr], xlp)
        send(("ix", 1, j), ig.at[0, oxh, c, oxl, :, fr], rix.at[1, :, fr], diag)

    def I0f(_):
        for j in range(PIECES):
            for n in range(3):
                arrive("ix", n, j)
        ig_out[:, cols(xh)] = (ig[0, xh, c, xl].astype(F32) + rix[0].astype(F32)).astype(BF16)
        ig_out[:, cols(oxh)] = (rix[1].astype(F32) + rix[2].astype(F32)).astype(BF16)

    steps = dict(
        R=R, Z=Z, T2=T2, T3=T3, F=F, A1=A1, B1a=B1a, B1b=B1b, B2=B2, A2=A2, A3=A3, A3x=A3x, A3y=A3y, B3=B3, B3x=B3x,
        B3y=B3y, A4=A4, A5a=A5a, A5b=A5b, B4x=B4x, B4y=B4y, B5=B5, CP=CP, C=C, G=G, Gp=Gp, Gr=Gr, Gl=Gl, I3=I3, I12=I12, I12b=I12b,
        I0=I0, I0f=I0f,
    )
    for step, *k in ORDER:
        steps[step](*k)
    for a in range(3):
        arrive("go", a)
    for cp in all_sends:
        cp.wait_send()
    assert not arrivals, "left over"


def write_out(a, b, c, d, ao, bo, co, do, sem):
    copies = []
    for i, (src, dst) in enumerate(((b, bo), (c, co), (d, do), (a, ao))):
        n = PIECES if src.shape[0] >= 16 * PIECES else 1
        step = src.shape[0] // n
        for j in range(n):
            part = pl.ds(j * step, step)
            cp = pltpu.make_async_copy(src.at[part], dst.at[part], sem.at[i, j])
            cp.start()
            copies.append(cp)
    for cp in copies:
        cp.wait()


def on_device(tokens, out_grad, gate_weight, up_weight, down_weight):
    rows, model = tokens.shape
    own_f, hidden = gate_weight.shape
    feats, half = 2 * own_f, hidden // 2
    q_cols = (half // 128 * 3 // 7) * 128
    p_cols = half - q_cols
    hr = rows // 2
    vmem = lambda *shape: pltpu.VMEM(shape, BF16)
    any_spec = pl.BlockSpec(memory_space=pl.ANY)
    out_shapes = [tokens, gate_weight, up_weight, down_weight]
    grads = pl.pallas_call(
        kernel,
        out_shape=[pltpu.VMEM(o.shape, BF16) for o in out_shapes],
        in_specs=[any_spec] * 5,
        out_specs=[pl.BlockSpec(memory_space=pltpu.VMEM)] * 4,
        scratch_shapes=[
            vmem(3, feats, half),
            vmem(4, 2, 2, 2, 2, rows, feats),
            vmem(2, 4, feats, 8 * rows),
            vmem(4, 4, 2, 3, rows, p_cols),
            vmem(4, 4, 2, 3, rows, q_cols),
            vmem(4, 2, 3, rows, p_cols),
            vmem(4, 2, 3, hr, q_cols),
            vmem(4, 2, 2, 3, rows, p_cols),
            vmem(4, 2, 3, rows, q_cols),
            vmem(4, 3, rows, p_cols),
            vmem(4, 4, 3, rows, q_cols),
            vmem(4, 4, 2, 3, rows, p_cols),
            vmem(4, 4, 2, 3, rows, q_cols),
            pltpu.VMEM((3, feats, half), F32),
            vmem(3, own_f, half),
            vmem(4, 2, 2, 2, rows, feats),
            vmem(4, 2, 2, rows, feats),
            vmem(2, 2, rows, feats),
            vmem(2, 2, 2, rows, feats),
            vmem(3, rows, feats),
            pltpu.VMEM((8 * rows, feats), F32),
            pltpu.SemaphoreType.DMA((N_SEM,)),
            pltpu.SemaphoreType.DMA((N_SEM,)),
            pltpu.SemaphoreType.DMA((16,)),
        ],
        compiler_params=pltpu.CompilerParams(
            collective_id=0, has_side_effects=True, vmem_limit_bytes=54 * 2**20
        ),
        cost_estimate=pl.CostEstimate(flops=15 * 10**9, bytes_accessed=12 * 2**20, transcendentals=10**6),
    )(tokens, out_grad, gate_weight, up_weight, down_weight)
    return pl.pallas_call(
        write_out,
        out_shape=[jax.ShapeDtypeStruct(o.shape, BF16) for o in out_shapes],
        in_specs=[any_spec] * 4,
        out_specs=[any_spec] * 4,
        scratch_shapes=[pltpu.SemaphoreType.DMA((4, PIECES))],
        compiler_params=pltpu.CompilerParams(vmem_limit_bytes=2 * 2**20),
        cost_estimate=pl.CostEstimate(flops=0, bytes_accessed=12 * 2**20, transcendentals=0),
    )(*grads)


def solution(mesh):
    in_specs = (
        P(("wt", "inp"), "out"),
        P(("wt", "inp"), "out"),
        P(("out", "wt"), "inp"),
        P(("out", "wt"), "inp"),
        P(("out", "wt"), "inp"),
    )
    out_specs = (
        P(("wt", "inp"), "out"),
        P(("out", "wt"), "inp"),
        P(("out", "wt"), "inp"),
        P(("out", "wt"), "inp"),
    )
    return jax.shard_map(
        on_device, mesh=mesh, in_specs=in_specs, out_specs=out_specs, check_vma=False
    )
```
